32 devices in a mesh: section: 2 (over core), seq: 4 (over y, x), tensor: 4 (over z).
Axes of the slice: x: 2, y: 2, z: 4, core: 2. Of those that a mesh axis runs over, the one named last changes fastest.
Arguments:
- queries: bfloat16 [2560, 8192], P(('section', 'seq'), 'tensor'), may hold values from -200 to 200
- neighbours: bfloat16 [10240, 8192], P(('section', 'seq', 'tensor')), may hold values from -6 to 6
- kv_weight: bfloat16 [2, 8192, 8192], P(None, None, 'tensor'), may hold values from -0.0625 to 0.0625
- out_weight: bfloat16 [8192, 8192], P('tensor'), may hold values from -0.5 to 0.5
- slot_map: int32 [40], replicated, may hold values from 0 to 39, as said below
Outputs:
- mixed: bfloat16 [2560, 8192], P(('section', 'seq', 'tensor'))
The draws below stay inside these ranges and needn't reach their ends.
Inputs may be any that keep to these rules, and one draw needn't show every extreme that they name: `slot_map`: distinct numbers; slot s lies on encoder shard s // 5; at most 2 spans of one sequence shard map to one encoder shard, and that many do for some pair of shards.
All inputs are finite; a program needn't handle non-finite values.
Results may differ from the reference program's by a relative error of at most 0.013.
Values may be sent and summed in bfloat16 or wider, within the bound.
A program may use at most 256 MiB of HBM per device.

```python
import math
import jax
import jax.numpy as jnp
from jax import lax

D = 8192
HEADS = 64
HD = 128
SPAN = 64
PEER = 2
CH_DEV = 5
CAPC = 5
KEYS = 256
GROUPS = 8
NCH = 40
SEQ = 2560


def draw_slot_map(key, part):
    key_seq = jax.random.fold_in(key, 11)
    key_enc = jax.random.fold_in(key, 12)
    key_order = jax.random.fold_in(key, 13)
    key_slots = jax.random.fold_in(key, 14)
    seq_perm = jax.random.permutation(key_seq, GROUPS).astype(jnp.int32)
    enc_perm = jax.random.permutation(key_enc, GROUPS).astype(jnp.int32)
    span_ids = jnp.arange(NCH, dtype=jnp.int32)
    shard = span_ids // CH_DEV
    order_score = jax.random.permutation(key_order, NCH).astype(jnp.int32)
    same_shard = shard[:, None] == shard[None, :]
    lower = order_score[None, :] < order_score[:, None]
    position = jnp.sum((same_shard & lower).astype(jnp.int32), axis=1).astype(jnp.int32)
    offset = position // PEER
    encoder = enc_perm[(seq_perm[shard] + offset) % GROUPS]
    slot_score = jax.random.permutation(key_slots, NCH).astype(jnp.int32)
    same_enc = encoder[:, None] == encoder[None, :]
    lower_slot = slot_score[None, :] < slot_score[:, None]
    rank = jnp.sum((same_enc & lower_slot).astype(jnp.int32), axis=1).astype(jnp.int32)
    return (encoder * CAPC + rank).astype(jnp.int32)


def draw_queries(key, part):
    key_main = jax.random.fold_in(key, 21)
    values = jnp.clip(jax.random.normal(key_main, (SEQ, D), jnp.float32), -6.0, 6.0)
    return values.astype(jnp.bfloat16)


def block_scale(own_key, shape, pieces, low, largest):
    level, own = 1.0, jax.random.fold_in(own_key, 6)
    for dim, blocks in pieces:
        draws = jnp.exp(jax.random.uniform(jax.random.fold_in(own, dim), (blocks,), jnp.float32, low / len(pieces), largest / len(pieces)))
        level = level * jnp.repeat(draws, shape[dim] // blocks).reshape([-1 if axis == dim else 1 for axis in range(len(shape))])
    return level


def scatter_about(own_key, dims, width, most, split=(), kind=jnp.bfloat16):
    result = jax.random.normal(own_key, dims, jnp.float32) * width
    if len(split) > 0:
        result = block_scale(own_key, dims, split, -0.22, 0.18) * result
    return jnp.clip(result, min=-most, max=most).astype(kind)


def setup_inputs(seed: int = 0) -> dict:
    key_of = jax.random.split(jax.random.key(seed), 6)
    return {
        "queries": draw_queries(jax.random.fold_in(key_of[5], 71), 0),
        "neighbours": scatter_about(key_of[1], (GROUPS * CAPC * KEYS, D), 1.0, 6.0, ((0, 32),)),
        "kv_weight": scatter_about(key_of[2], (2, D, D), D ** -0.5, 0.0625, ((2, 4),)),
        "out_weight": scatter_about(key_of[3], (D, D), HD ** -0.5, 0.5, ((0, 4),)),
        "slot_map": draw_slot_map(jax.random.fold_in(key_of[5], 71), 0),
    }


def reference(queries, neighbours, kv_weight, out_weight, slot_map):
    span_rows = neighbours.reshape(GROUPS * CAPC, KEYS, D)[slot_map].reshape(NCH * KEYS, D)
    keys = jnp.dot(span_rows, kv_weight[0], preferred_element_type=jnp.float32).astype(jnp.bfloat16)
    values = jnp.dot(span_rows, kv_weight[1], preferred_element_type=jnp.float32).astype(jnp.bfloat16)
    keys = keys.reshape(NCH, KEYS, HEADS, HD).astype(jnp.float32)
    values = values.reshape(NCH, KEYS, HEADS, HD).astype(jnp.float32)
    query_heads = queries.reshape(NCH, SPAN, HEADS, HD).astype(jnp.float32)
    scores = jnp.einsum('cqhd,ckhd->chqk', query_heads, keys) * (1.0 / math.sqrt(HD))
    peak = lax.optimization_barrier(jnp.max(scores, axis=-1, keepdims=True))
    expo = jnp.exp(scores - peak)
    weights = (expo / lax.optimization_barrier(jnp.sum(expo, axis=-1, keepdims=True))).astype(jnp.bfloat16)
    attended = jnp.einsum('chqk,ckhd->cqhd', weights.astype(jnp.float32), values)
    attended = attended.astype(jnp.bfloat16).reshape(SEQ, D)
    return jnp.dot(attended, out_weight, preferred_element_type=jnp.float32).astype(jnp.bfloat16)
```

```python
import math

import jax
import jax.numpy as jnp
from jax import lax
from jax.experimental import pallas as pl
from jax.experimental.pallas import tpu as pltpu
from jax.sharding import PartitionSpec as P

HD = 128
SPAN = 64
PEER = 2
CH_DEV = 5
CAPC = 5
KEYS = 256
HEADS_STEP = 4
PARTS = 2
OUTER = ("section", "seq")


def attend_kernel(q_ref, k_ref, v_ref, o_ref):
    for h in range(q_ref.shape[2] // HD):
        cols = slice(h * HD, (h + 1) * HD)
        scores = lax.dot_general(
            q_ref[0, :, cols],
            k_ref[:, cols],
            (((1,), (1,)), ((), ())),
            preferred_element_type=jnp.float32,
        ) * (1.0 / math.sqrt(HD))
        peak = jnp.max(scores, axis=-1, keepdims=True)
        expo = jnp.exp(scores - peak)
        weights = (expo / jnp.sum(expo, axis=-1, keepdims=True)).astype(jnp.bfloat16)
        o_ref[0, :, cols] = jnp.dot(
            weights, v_ref[:, cols], preferred_element_type=jnp.float32
        ).astype(o_ref.dtype)


def attend(query_blocks, key_values):
    slots, span, width = query_blocks.shape
    step = math.gcd(HEADS_STEP * HD, width)
    steps = width // step
    return pl.pallas_call(
        attend_kernel,
        grid=(slots, steps),
        in_specs=[
            pl.BlockSpec((1, span, step), lambda s, h: (s, 0, h)),
            pl.BlockSpec((KEYS, step), lambda s, h: (s, h)),
            pl.BlockSpec((KEYS, step), lambda s, h: (s, h + steps)),
        ],
        out_specs=pl.BlockSpec((1, span, step), lambda s, h: (s, 0, h)),
        out_shape=jax.ShapeDtypeStruct(query_blocks.shape, jnp.bfloat16),
        cost_estimate=pl.CostEstimate(
            flops=4 * slots * span * KEYS * width,
            bytes_accessed=4 * slots * (span + KEYS) * width,
            transcendentals=slots * span * KEYS * (width // HD),
        ),
    )(query_blocks, key_values, key_values)


def pick(array, index, count):
    return jnp.concatenate(
        [lax.dynamic_slice_in_dim(array, index[i], 1, 0) for i in range(count)], axis=0
    )


def on_device(queries, neighbours, kv_weight, out_weight, slot_map):
    groups = lax.axis_size(OUTER)
    tensors = lax.axis_size("tensor")
    group = lax.axis_index(OUTER)
    width = kv_weight.shape[2]
    spans = slot_map.shape[0]
    depth = neighbours.shape[1]

    span_ids = jnp.arange(spans, dtype=jnp.int32)
    owner_shard = slot_map // CAPC
    seq_owner = span_ids // CH_DEV
    earlier = (seq_owner[:, None] == seq_owner[None, :]) & (
        owner_shard[:, None] == owner_shard[None, :]
    )
    earlier = earlier & (span_ids[None, :] < span_ids[:, None])
    arrival = jnp.sum(earlier.astype(jnp.int32), axis=1)
    peers = jnp.arange(groups * PEER, dtype=jnp.int32)[:, None]
    out_hit = (owner_shard * PEER + arrival)[None, :] == peers
    out_hit = out_hit & (seq_owner == group)[None, :]
    ask = jnp.sum(jnp.where(out_hit, (span_ids % CH_DEV)[None, :], 0), axis=1)
    back_hit = (seq_owner * PEER + arrival)[None, :] == peers
    back_hit = back_hit & (owner_shard == group)[None, :]
    answer = jnp.sum(jnp.where(back_hit, (slot_map % CAPC)[None, :], 0), axis=1)
    slots = group * CAPC + jnp.arange(CAPC, dtype=jnp.int32)[:, None]
    asked = jnp.sum(
        jnp.where(slot_map[None, :] == slots, (seq_owner * PEER + arrival)[None, :], 0),
        axis=1,
    )
    own = group * CH_DEV + jnp.arange(CH_DEV, dtype=jnp.int32)[:, None]
    answered = jnp.sum(
        jnp.where(span_ids[None, :] == own, (owner_shard * PEER + arrival)[None, :], 0),
        axis=1,
    )

    rows_out = queries.shape[0] // tensors
    run = math.gcd(rows_out, SPAN) // PARTS
    query_rows = queries.reshape(CH_DEV, SPAN // (run * PARTS), PARTS, run, width)
    query_rows = query_rows.transpose(0, 2, 1, 3, 4).reshape(CH_DEV, SPAN, width)
    sent = pick(query_rows, ask, groups * PEER)
    got = lax.all_to_all(sent, OUTER, split_axis=0, concat_axis=0, tiled=True)
    query_blocks = pick(got, asked, CAPC)

    pieces = CAPC
    unit = neighbours.shape[0] // pieces
    key_values = jnp.zeros((tensors, pieces, unit, 2 * width), jnp.bfloat16)
    for i in range(pieces):
        block = lax.all_gather(
            neighbours[i * unit : (i + 1) * unit], "tensor", axis=0, tiled=True
        )
        part = jnp.einsum("rd,kde->rke", block, kv_weight, preferred_element_type=jnp.float32)
        part = part.astype(jnp.bfloat16).reshape(tensors, 1, unit, 2 * width)
        key_values = lax.dynamic_update_slice(key_values, part, (0, i, 0, 0))
    key_values = key_values.reshape(CAPC * KEYS, 2 * width)

    attended = attend(query_blocks, key_values)

    outs = []
    part_rows = SPAN // PARTS
    for c in range(PARTS):
        piece = attended[:, c * part_rows : (c + 1) * part_rows]
        back = lax.all_to_all(
            pick(piece, answer, groups * PEER), OUTER, split_axis=0, concat_axis=0, tiled=True
        )
        mine = pick(back, answered, CH_DEV).reshape(CH_DEV * part_rows, width)
        total = jnp.dot(mine, out_weight, preferred_element_type=jnp.float32)
        outs.append(
            lax.psum_scatter(
                total.astype(jnp.bfloat16), "tensor", scatter_dimension=0, tiled=True
            ).reshape(rows_out // (run * PARTS), 1, run, depth)
        )
    return jnp.concatenate(outs, axis=1).reshape(rows_out, depth)


def solution(mesh):
    placed = (
        P(("section", "seq"), "tensor"),
        P(("section", "seq", "tensor"), None),
        P(None, None, "tensor"),
        P("tensor", None),
        P(),
    )
    return jax.shard_map(
        on_device,
        mesh=mesh,
        in_specs=placed,
        out_specs=P(("section", "seq", "tensor"), None),
        check_vma=False,
    )
```

```python
import functools
import math

import jax
import jax.numpy as jnp
from jax import lax
from jax.experimental import pallas as pl
from jax.experimental.pallas import tpu as pltpu
from jax.sharding import PartitionSpec as P

HD = 128
SPAN = 64
PEER = 2
CH_DEV = 5
CAPC = 5
KEYS = 256
HEADS_STEP = 2
FIRST = 4
PARTS = 2
OUTER = ("section", "seq")


def attend_kernel(unit, first, rows_ref, weight_ref, before_ref, query_ref, *out_refs):
    rows = rows_ref[...]
    last = [
        jnp.dot(rows, weight_ref[k], preferred_element_type=jnp.float32).astype(jnp.bfloat16)
        for k in range(2)
    ]
    part_rows = SPAN // len(out_refs)
    for s in range(CAPC):
        key_value = []
        for k in range(2):
            runs = []
            for u in range(s * (KEYS // unit), (s + 1) * (KEYS // unit)):
                t, i = divmod(u, CAPC)
                if i < first:
                    at = (t * first + i) * unit
                    runs.append(before_ref[k, at : at + unit])
                else:
                    at = (t * (CAPC - first) + i - first) * unit
                    runs.append(last[k][at : at + unit])
            key_value.append(jnp.concatenate(runs, axis=0))
        keys, values = key_value
        query = query_ref[s]
        for h in range(query_ref.shape[2] // HD):
            cols = slice(h * HD, (h + 1) * HD)
            scores = lax.dot_general(
                query[:, cols],
                keys[:, cols],
                (((1,), (1,)), ((), ())),
                preferred_element_type=jnp.float32,
            ) * (1.0 / math.sqrt(HD))
            peak = jnp.max(scores, axis=-1, keepdims=True)
            expo = jnp.exp(scores - peak)
            weights = (expo / jnp.sum(expo, axis=-1, keepdims=True)).astype(jnp.bfloat16)
            result = jnp.dot(weights, values[:, cols], preferred_element_type=jnp.float32)
            result = result.astype(jnp.bfloat16)
            for c, o_ref in enumerate(out_refs):
                o_ref[s, :, cols] = result[c * part_rows : (c + 1) * part_rows]


def attend(rows, kv_weight, before, queries, unit, first):
    peers, span, width = queries.shape
    depth = rows.shape[1]
    step = math.gcd(HEADS_STEP * HD, width)
    part = (peers, span // PARTS, step)
    spec = dict(
        grid=(width // step,),
        in_specs=[
            pl.BlockSpec(rows.shape, lambda h: (0, 0)),
            pl.BlockSpec((2, depth, step), lambda h: (0, 0, h)),
            pl.BlockSpec((2, before.shape[1], step), lambda h: (0, 0, h)),
            pl.BlockSpec((peers, span, step), lambda h: (0, 0, h)),
        ],
        out_specs=[pl.BlockSpec(part, lambda h: (0, 0, h))] * PARTS,
    )
    made = jax.ShapeDtypeStruct((peers, span // PARTS, width), jnp.bfloat16)
    return pl.pallas_call(
        functools.partial(attend_kernel, unit, first),
        **spec,
        out_shape=[made] * PARTS,
        compiler_params=pltpu.CompilerParams(vmem_limit_bytes=52 * 2**20),
        cost_estimate=pl.CostEstimate(
            flops=4 * rows.shape[0] * depth * width + 4 * CAPC * span * KEYS * width,
            bytes_accessed=4 * depth * width + 2 * rows.size + 2 * before.size,
            transcendentals=CAPC * span * KEYS * (width // HD),
        ),
    )(rows, kv_weight, before, queries)


def pick(array, index, count):
    return jnp.concatenate(
        [lax.dynamic_slice_in_dim(array, index[i], 1, 0) for i in range(count)], axis=0
    )


def on_device(queries, neighbours, kv_weight, out_weight, slot_map):
    groups = lax.axis_size(OUTER)
    tensors = lax.axis_size("tensor")
    group = lax.axis_index(OUTER)
    width = kv_weight.shape[2]
    spans = slot_map.shape[0]
    depth = neighbours.shape[1]

    span_ids = jnp.arange(spans, dtype=jnp.int32)
    owner_shard = slot_map // CAPC
    seq_owner = span_ids // CH_DEV
    earlier = (seq_owner[:, None] == seq_owner[None, :]) & (
        owner_shard[:, None] == owner_shard[None, :]
    )
    earlier = earlier & (span_ids[None, :] < span_ids[:, None])
    arrival = jnp.sum(earlier.astype(jnp.int32), axis=1)
    peers = jnp.arange(groups * PEER, dtype=jnp.int32)[:, None]
    out_hit = (owner_shard * PEER + arrival)[None, :] == peers
    out_hit = out_hit & (seq_owner == group)[None, :]
    ask = jnp.sum(jnp.where(out_hit, (span_ids % CH_DEV)[None, :], 0), axis=1)
    back_hit = (seq_owner * PEER + arrival)[None, :] == peers
    back_hit = back_hit & (owner_shard == group)[None, :]
    answer = jnp.sum(jnp.where(back_hit, (slot_map % CAPC)[None, :], 0), axis=1)
    slots = group * CAPC + jnp.arange(CAPC, dtype=jnp.int32)[:, None]
    asked = jnp.sum(
        jnp.where(slot_map[None, :] == slots, (seq_owner * PEER + arrival)[None, :], 0),
        axis=1,
    )
    own = group * CH_DEV + jnp.arange(CH_DEV, dtype=jnp.int32)[:, None]
    answered = jnp.sum(
        jnp.where(span_ids[None, :] == own, (owner_shard * PEER + arrival)[None, :], 0),
        axis=1,
    )

    rows_out = queries.shape[0] // tensors
    run = math.gcd(rows_out, SPAN) // PARTS
    query_rows = queries.reshape(CH_DEV, SPAN // (run * PARTS), PARTS, run, width)
    query_rows = query_rows.transpose(0, 2, 1, 3, 4).reshape(CH_DEV, SPAN, width)
    sent = pick(query_rows, ask, groups * PEER)
    got = lax.all_to_all(sent, OUTER, split_axis=0, concat_axis=0, tiled=True)

    unit = neighbours.shape[0] // CAPC
    block = lax.all_gather(neighbours[: FIRST * unit], "tensor", axis=0, tiled=True)
    rest = lax.all_gather(neighbours[FIRST * unit :], "tensor", axis=0, tiled=True)
    before = jnp.einsum("rd,kde->kre", block, kv_weight, preferred_element_type=jnp.float32)
    before = before.astype(jnp.bfloat16)
    attended = attend(
        rest, kv_weight, before, pick(got, asked, CAPC), unit, FIRST
    )

    outs = []
    part_rows = SPAN // PARTS
    for c in range(PARTS):
        back = lax.all_to_all(
            pick(attended[c], answer, groups * PEER), OUTER, split_axis=0, concat_axis=0, tiled=True
        )
        mine = pick(back, answered, CH_DEV).reshape(CH_DEV * part_rows, width)
        total = jnp.dot(mine, out_weight, preferred_element_type=jnp.float32)
        outs.append(
            lax.psum_scatter(
                total.astype(jnp.bfloat16), "tensor", scatter_dimension=0, tiled=True
            ).reshape(rows_out // (run * PARTS), 1, run, depth)
        )
    return jnp.concatenate(outs, axis=1).reshape(rows_out, depth)


def solution(mesh):
    placed = (
        P(("section", "seq"), "tensor"),
        P(("section", "seq", "tensor"), None),
        P(None, None, "tensor"),
        P("tensor", None),
        P(),
    )
    return jax.shard_map(
        on_device,
        mesh=mesh,
        in_specs=placed,
        out_specs=P(("section", "seq", "tensor"), None),
        check_vma=False,
    )
```
